32 devices in a mesh: frames: 4 (over y, core), space: 8 (over z, x).
Axes of the slice: x: 2, y: 2, z: 4, core: 2. Of those that a mesh axis runs over, the one named last changes fastest.
Arguments:
- latent: bfloat16 [4, 16, 256, 1152], P('frames', 'space'), may hold values from -6 to 6
- query_rows: bfloat16 [4, 16, 256, 1152], P('frames', 'space'), may hold values from -5.5 to 5.5
- key_rows: bfloat16 [4, 16, 256, 1152], P('frames', 'space'), may hold values from -5.5 to 5.5
- value_rows: bfloat16 [4, 16, 256, 1152], P('frames', 'space'), may hold values from -6 to 6
- cached_out: bfloat16 [4, 16, 256, 1152], P('frames', 'space'), may hold values from -4 to 4
- refreshed: int32 [4, 16], P('frames', 'space'), may hold values from 0 to 1, as said below
- band_width: int32 [16], replicated, may hold values from 1 to 3, as said below
- out_weight: bfloat16 [1152, 1152], replicated, may hold values from -0.1875 to 0.1875
- temporal_weight: bfloat16 [1152, 3456], replicated, may hold values from -0.1360803 to 0.1360803
Outputs:
- mixed: bfloat16 [4, 16, 256, 1152], P('frames', 'space')
The draws below stay inside these ranges and needn't reach their ends.
Inputs may be any that keep to these rules, and one draw needn't show every extreme that they name: `refreshed`: 1 marks a tile that is recomputed; tiles further down a frame are recomputed more often. `band_width`: at least one head reaches 3 frames.
All inputs are finite; a program needn't handle non-finite values.
Results may differ from the reference program's by a relative error of at most 0.008.
Values may be sent and summed in bfloat16 or wider, within the bound.
A program may use at most 128 MiB of HBM per device.

```python
import math
import jax
import jax.numpy as jnp
from jax import lax

D = 1152
HEADS = 16
TILE_TOK = 256
EDGE = 64
FRAMES = 4
TILES = 16


def drawn_pair(key):
    shape_full = (FRAMES, TILES, TILE_TOK, D)
    query = jnp.clip(jax.random.normal(jax.random.fold_in(key, 11), shape_full, jnp.float32), -5.5, 5.5)
    keys = jnp.clip(jax.random.normal(jax.random.fold_in(key, 12), shape_full, jnp.float32), -5.5, 5.5)
    return (query, keys)


def draw_query_rows(key, part):
    return drawn_pair(key)[0].astype(jnp.bfloat16)


def draw_key_rows(key, part):
    return drawn_pair(key)[1].astype(jnp.bfloat16)


def draw_latent(key, part):
    shape_full = (FRAMES, TILES, TILE_TOK, D)
    base = jnp.clip(jax.random.normal(jax.random.fold_in(key, 31), shape_full, jnp.float32), -6.0, 6.0)
    return base.astype(jnp.bfloat16)


def draw_temporal_weight(key, part):
    base = jnp.clip(jax.random.normal(jax.random.fold_in(key, 41), (D, 3 * D), jnp.float32), -4.0, 4.0) / math.sqrt(D)
    return base.astype(jnp.bfloat16)


def draw_refreshed(key, part):
    level = jax.random.randint(key, (FRAMES, TILES), 0, 8)
    threshold = 1 + 6 * jnp.arange(TILES, dtype=jnp.int32) // TILES
    return (level < threshold[None, :]).astype(jnp.int32)


def draw_band_width(key, part):
    widest = jax.random.randint(jax.random.fold_in(key, 51), (), 0, HEADS)
    reach = jax.random.randint(jax.random.fold_in(key, 52), (HEADS,), 1, FRAMES)
    return jnp.where(jnp.arange(HEADS, dtype=jnp.int32) == widest, FRAMES - 1, reach).astype(jnp.int32)


def block_levels(key, dims, pieces, low, high):
    gain = 1.0
    for axis_at, blocks in pieces:
        heights = jax.random.uniform(jax.random.fold_in(jax.random.fold_in(key, 6), axis_at), (blocks,), jnp.float32, low / len(pieces), high / len(pieces))
        gain = gain * jnp.repeat(jnp.exp(heights), dims[axis_at] // blocks).reshape((-1,) + (1,) * (len(dims) - 1 - axis_at))
    return gain


def gaussian(rng, dims, spread, limit, split=(), held_as=jnp.bfloat16):
    gain = block_levels(rng, dims, split, -0.22, 0.18) if split else 1.0
    entries = jax.random.normal(rng, dims, jnp.float32) * spread * gain
    return jnp.minimum(jnp.maximum(entries, -limit), limit).astype(held_as)


def setup_inputs(seed: int = 0) -> dict:
    streams_of = jax.random.split(jax.random.key(seed), 10)
    latent = draw_latent(jax.random.fold_in(streams_of[9], 71), 0)
    query_rows = draw_query_rows(jax.random.fold_in(streams_of[9], 71), 0)
    key_rows = draw_key_rows(jax.random.fold_in(streams_of[9], 71), 0)
    value_rows = gaussian(streams_of[3], (FRAMES, TILES, TILE_TOK, D), 1.0, 6.0, ((0, 4), (1, 8)))
    cached_out = gaussian(streams_of[4], (FRAMES, TILES, TILE_TOK, D), 0.3, 4.0, ((0, 4), (1, 8)))
    refreshed = draw_refreshed(jax.random.fold_in(streams_of[9], 71), 0)
    band_width = draw_band_width(jax.random.fold_in(streams_of[9], 71), 0)
    out_weight = gaussian(streams_of[7], (D, D), D ** -0.5, 0.1875)
    temporal_weight = draw_temporal_weight(jax.random.fold_in(streams_of[9], 71), 0)
    return {"latent": latent, "query_rows": query_rows, "key_rows": key_rows, "value_rows": value_rows, "cached_out": cached_out, "refreshed": refreshed, "band_width": band_width, "out_weight": out_weight, "temporal_weight": temporal_weight}


def soft_rows(scores):
    top = lax.optimization_barrier(jnp.max(scores, axis=-1, keepdims=True))
    expo = jnp.exp(scores - top)
    return expo / lax.optimization_barrier(jnp.sum(expo, axis=-1, keepdims=True))

def temporal_block(block, band_width, head_count, width):
    adim, sdim, bdim, idim, pdim, _ = block.shape
    head_dim = width // head_count
    scaling = 1.0 / math.sqrt(head_dim)
    query6 = block[..., :width].reshape(adim, sdim, bdim, idim, pdim, head_count, head_dim).astype(jnp.float32)
    key6 = block[..., width:2 * width].reshape(adim, sdim, bdim, idim, pdim, head_count, head_dim).astype(jnp.float32)
    value6 = block[..., 2 * width:].reshape(adim, sdim, bdim, idim, pdim, head_count, head_dim).astype(jnp.float32)
    scores = jnp.einsum('asbiphe,csuiphe->siphabcu', query6, key6) * scaling
    frame_index = jnp.arange(adim, dtype=jnp.int32)[:, None] * bdim + jnp.arange(bdim, dtype=jnp.int32)[None, :]
    frame_gap = jnp.abs(frame_index[:, :, None, None] - frame_index[None, None, :, :])
    allowed = frame_gap[None] <= band_width[:, None, None, None, None]
    scores = jnp.where(allowed, scores, -jnp.inf)
    flat_scores = scores.reshape(sdim, idim, pdim, head_count, adim, bdim, adim * bdim)
    weights = soft_rows(flat_scores).astype(jnp.bfloat16)
    weights = weights.reshape(sdim, idim, pdim, head_count, adim, bdim, adim, bdim).astype(jnp.float32)
    result = jnp.einsum('siphabcu,csuiphe->asbiphe', weights, value6)
    return result.astype(jnp.bfloat16).reshape(adim * sdim * bdim, idim, pdim, width)

def spatial_frame(items, out_weight, temporal_weight):
    latent, query_rows, key_rows, value_rows, cached_out, refreshed = items
    tile_count, tok_count, width = latent.shape
    head_count = HEADS
    head_dim = width // head_count
    scaling = 1.0 / math.sqrt(head_dim)
    zero_edge = jnp.zeros((1, EDGE, width), jnp.bfloat16)
    prev_key = jnp.concatenate([zero_edge, key_rows[:-1, -EDGE:]], axis=0)
    next_key = jnp.concatenate([key_rows[1:, :EDGE], zero_edge], axis=0)
    prev_value = jnp.concatenate([zero_edge, value_rows[:-1, -EDGE:]], axis=0)
    next_value = jnp.concatenate([value_rows[1:, :EDGE], zero_edge], axis=0)
    key_ext = jnp.concatenate([prev_key, key_rows, next_key], axis=1)
    value_ext = jnp.concatenate([prev_value, value_rows, next_value], axis=1)
    span = tok_count + 2 * EDGE
    position = jnp.arange(span, dtype=jnp.int32)
    tile_index = jnp.arange(tile_count, dtype=jnp.int32)[:, None]
    usable = ((position[None, :] >= EDGE) | (tile_index > 0)) & ((position[None, :] < EDGE + tok_count) | (tile_index < tile_count - 1))
    query5 = query_rows.reshape(tile_count, tok_count, head_count, head_dim).astype(jnp.float32)
    key5 = key_ext.reshape(tile_count, span, head_count, head_dim).astype(jnp.float32)
    value5 = value_ext.reshape(tile_count, span, head_count, head_dim).astype(jnp.float32)
    scores = jnp.einsum('tqhe,tkhe->thqk', query5, key5) * scaling
    scores = jnp.where(usable[:, None, None, :], scores, -jnp.inf)
    weights = soft_rows(scores).astype(jnp.bfloat16).astype(jnp.float32)
    fresh = jnp.einsum('thqk,tkhe->tqhe', weights, value5).astype(jnp.bfloat16).reshape(tile_count, tok_count, width)
    spatial = jnp.where(refreshed[:, None, None] == 1, fresh, cached_out)
    projected = jnp.dot(spatial.reshape(-1, width), out_weight, preferred_element_type=jnp.float32)
    hidden = (latent.astype(jnp.float32) + projected.reshape(tile_count, tok_count, width)).astype(jnp.bfloat16)
    hidden32 = hidden.astype(jnp.float32)
    normed = (hidden32 * lax.rsqrt(lax.optimization_barrier(jnp.mean(hidden32 * hidden32, axis=-1, keepdims=True)) + 1e-06)).astype(jnp.bfloat16)
    packed = jnp.dot(normed.reshape(-1, width), temporal_weight, preferred_element_type=jnp.float32).astype(jnp.bfloat16)
    return (hidden, packed.reshape(tile_count, tok_count, 3 * width))

def reference(latent, query_rows, key_rows, value_rows, cached_out, refreshed, band_width, out_weight, temporal_weight):
    width = latent.shape[-1]
    hidden, packed = lax.map(lambda items: spatial_frame(items, out_weight, temporal_weight), (latent, query_rows, key_rows, value_rows, cached_out, refreshed))
    by_tile = jnp.moveaxis(packed, 1, 0)

    def one_tile(block):
        frame_count, tok_count, _ = block.shape
        result = temporal_block(block.reshape(1, 1, frame_count, 1, tok_count, 3 * width), band_width, HEADS, width)
        return result.reshape(frame_count, tok_count, width)
    temporal = jnp.moveaxis(lax.map(one_tile, by_tile), 0, 1)
    return (hidden.astype(jnp.float32) + temporal.astype(jnp.float32)).astype(jnp.bfloat16)
```

```python
import functools
import math

import jax
import jax.numpy as jnp
from jax import lax
from jax.experimental import pallas as pl
from jax.experimental.pallas import tpu as pltpu
from jax.sharding import PartitionSpec as P

EDGE = 64
LANES = 128
MESH = pl.DeviceIdType.MESH


def kernel(
    frames,
    groups,
    heads,
    latent_hbm,
    query_hbm,
    key_hbm,
    value_hbm,
    cached_hbm,
    refreshed_ref,
    band_ref,
    out_weight_hbm,
    temporal_weight_hbm,
    mixed_ref,
    query,
    key,
    value,
    latent,
    cached,
    out_weight,
    temporal_weight,
    spatial,
    hidden,
    normed,
    arrived,
    packed,
    attended,
    returned,
    gather,
    spread,
    load_sem,
    edge_send,
    edge_recv,
    norm_send,
    norm_recv,
    back_send,
    back_recv,
):
    _, tiles, rows, width = latent_hbm.shape
    share = rows // frames
    span = rows + 2 * EDGE
    head_dim = width // heads
    me = lax.axis_index("frames")
    at = lax.axis_index("space")
    has_above = at > 0
    has_below = at < groups - 1

    loads = []

    def load(src, dst):
        copy = pltpu.make_async_copy(src, dst, load_sem.at[len(loads)])
        copy.start()
        loads.append(copy)

    for t in range(tiles):
        load(query_hbm.at[0, t], query.at[t])
        for src, dst in ((key_hbm, key), (value_hbm, value)):
            load(src.at[0, t], dst.at[t, pl.ds(EDGE, rows)])
            if t > 0:
                load(src.at[0, t - 1, pl.ds(rows - EDGE, EDGE)], dst.at[t, pl.ds(0, EDGE)])
            if t < tiles - 1:
                load(src.at[0, t + 1, pl.ds(0, EDGE)], dst.at[t, pl.ds(rows + EDGE, EDGE)])
    load(cached_hbm.at[0], cached)
    load(latent_hbm.at[0], latent)
    load(out_weight_hbm, out_weight)
    early = len(loads)
    load(temporal_weight_hbm, temporal_weight)

    barrier = pltpu.get_barrier_semaphore()
    for d in range(1, frames):
        pl.semaphore_signal(
            barrier, inc=1, device_id={"frames": lax.rem(me + d, frames)}, device_id_type=MESH
        )

    @pl.when(has_above)
    def _():
        pl.semaphore_signal(barrier, inc=1, device_id={"space": at - 1}, device_id_type=MESH)

    @pl.when(has_below)
    def _():
        pl.semaphore_signal(barrier, inc=1, device_id={"space": at + 1}, device_id_type=MESH)

    peers = frames - 1 + jnp.where(has_above, 1, 0) + jnp.where(has_below, 1, 0)
    pl.semaphore_wait(barrier, peers)

    def edge(i, which, target):
        src, dst = ((key_hbm, key), (value_hbm, value))[i]
        if which == 0:
            source = src.at[0, tiles - 1, pl.ds(rows - EDGE, EDGE)]
            place = dst.at[0, pl.ds(0, EDGE)]
        else:
            source = src.at[0, 0, pl.ds(0, EDGE)]
            place = dst.at[tiles - 1, pl.ds(rows + EDGE, EDGE)]
        return pltpu.make_async_remote_copy(
            src_ref=source,
            dst_ref=place,
            send_sem=edge_send.at[which, i],
            recv_sem=edge_recv.at[which, i],
            device_id={"space": target},
            device_id_type=MESH,
        )

    @pl.when(has_below)
    def _():
        for i in range(2):
            edge(i, 0, at + 1).start()

    @pl.when(has_above)
    def _():
        for i in range(2):
            edge(i, 1, at - 1).start()

    @pl.when(jnp.logical_not(has_above))
    def _():
        for dst in (key, value):
            dst[0, pl.ds(0, EDGE)] = jnp.zeros((EDGE, width), dst.dtype)

    @pl.when(jnp.logical_not(has_below))
    def _():
        for dst in (key, value):
            dst[tiles - 1, pl.ds(rows + EDGE, EDGE)] = jnp.zeros((EDGE, width), dst.dtype)

    column = lax.broadcasted_iota(jnp.int32, (width, LANES), 0)
    first = lax.broadcasted_iota(jnp.int32, (width, LANES), 1) * head_dim
    inside = jnp.where((column >= first) & (column < first + head_dim), 1.0, 0.0)
    gather[...] = inside.astype(jnp.bfloat16)
    column = lax.broadcasted_iota(jnp.int32, (LANES, width), 1)
    first = lax.broadcasted_iota(jnp.int32, (LANES, width), 0) * head_dim
    inside = jnp.where((column >= first) & (column < first + head_dim), 1.0, 0.0)
    spread[...] = inside.astype(jnp.bfloat16)
    lane = lax.broadcasted_iota(jnp.int32, (1, LANES), 1)
    band = jnp.zeros((1, LANES), jnp.int32)
    for h in range(heads):
        band = jnp.where(lane == h, band_ref[h], band)

    for copy in loads[:early]:
        copy.wait()

    @pl.when(has_above)
    def _():
        for i in range(2):
            edge(i, 0, at - 1).wait_recv()

    @pl.when(has_below)
    def _():
        for i in range(2):
            edge(i, 1, at + 1).wait_recv()

    scale = math.log2(math.e) / math.sqrt(head_dim)
    position = lax.broadcasted_iota(jnp.int32, (1, span), 1)

    def norm_copy(t, d):
        peer = lax.rem(me + d, frames)
        return pltpu.make_async_remote_copy(
            src_ref=normed.at[t, peer],
            dst_ref=arrived.at[t, me],
            send_sem=norm_send.at[t, d],
            recv_sem=norm_recv.at[t, d],
            device_id={"frames": peer},
            device_id_type=MESH,
        )

    def back_copy(t, d):
        peer = lax.rem(me + d, frames)
        return pltpu.make_async_remote_copy(
            src_ref=attended.at[t, peer],
            dst_ref=returned.at[t, me],
            send_sem=back_send.at[t, d],
            recv_sem=back_recv.at[t, d],
            device_id={"frames": peer},
            device_id_type=MESH,
        )

    def spatial_tile(t, carry):
        whole = at * tiles + t
        low = jnp.where(whole == 0, EDGE, 0)
        high = jnp.where(whole == groups * tiles - 1, rows + EDGE, span)
        bias = jnp.where((position >= low) & (position < high), 0.0, -jnp.inf)
        fresh_here = refreshed_ref[0, t] == 1
        partial = None
        for h in range(heads):
            start, stop = h * head_dim, (h + 1) * head_dim
            a, b = start // LANES, -(-stop // LANES)
            cols = slice(a * LANES, b * LANES)
            at_col = lax.broadcasted_iota(jnp.int32, (1, (b - a) * LANES), 1) + a * LANES
            mine = (at_col >= start) & (at_col < stop)
            q = query[t, :, cols] * jnp.where(mine, 1.0, 0.0).astype(jnp.bfloat16)
            scores = lax.dot_general(
                q, key[t, :, cols], (((1,), (1,)), ((), ())), preferred_element_type=jnp.float32
            )
            scores = scores + bias
            top = jnp.max(scores, axis=-1, keepdims=True)
            expo = jnp.exp2((scores - top) * scale)
            total = jnp.sum(expo, axis=-1, keepdims=True)
            out = jnp.dot(
                expo.astype(jnp.bfloat16), value[t, :, cols], preferred_element_type=jnp.float32
            )
            out = out * (1.0 / total)
            for block in range(a, b):
                piece = out[:, (block - a) * LANES : (block - a + 1) * LANES]
                if start > block * LANES:
                    piece = jnp.where(lane + block * LANES >= start, piece, partial)
                if stop >= (block + 1) * LANES:
                    old = cached[t, :, block * LANES : (block + 1) * LANES]
                    spatial[:, block * LANES : (block + 1) * LANES] = jnp.where(
                        fresh_here, piece.astype(jnp.bfloat16), old
                    )
                else:
                    partial = piece
        projected = jnp.dot(spatial[...], out_weight[...], preferred_element_type=jnp.float32)
        hid = (latent[t].astype(jnp.float32) + projected).astype(jnp.bfloat16)
        hidden[t] = hid
        hid32 = hid.astype(jnp.float32)
        mean = jnp.mean(hid32 * hid32, axis=-1, keepdims=True)
        norm = (hid32 * lax.rsqrt(mean + 1e-06)).astype(jnp.bfloat16)
        normed[t] = norm.reshape(frames, share, width)
        for d in range(1, frames):
            norm_copy(t, frames - d).start()
        arrived[t, me] = normed[t, me]
        return carry

    lax.fori_loop(0, tiles, spatial_tile, 0)
    loads[early].wait()

    def temporal_tile(t, carry):
        for d in range(1, frames):
            norm_in(t, d)
        block = arrived[t].reshape(frames * share, width)

        def project(j, c):
            w = temporal_weight[:, pl.ds(pl.multiple_of(j * width, LANES), width)]
            flat = jnp.dot(block, w, preferred_element_type=jnp.float32).astype(jnp.bfloat16)
            packed[j] = flat.reshape(frames, share, width)
            return c

        lax.fori_loop(0, 3, project, 0)
        for d in range(1, frames + 1):
            f = lax.rem(me + frames - d, frames)
            products = packed[0, f][None] * packed[1]
            scores = jnp.dot(
                products.reshape(frames * share, width),
                gather[...],
                preferred_element_type=jnp.float32,
            ).reshape(frames, share, LANES)
            scores = [
                jnp.where(jnp.abs(f - g) <= band, scores[g], -jnp.inf) for g in range(frames)
            ]
            top = functools.reduce(jnp.maximum, scores)
            expo = [jnp.exp2((s - top) * scale) for s in scores]
            inverse = 1.0 / functools.reduce(jnp.add, expo)
            weights = jnp.stack([(e * inverse).astype(jnp.bfloat16) for e in expo])
            wide = jnp.dot(
                weights.reshape(frames * share, LANES),
                spread[...],
                preferred_element_type=jnp.float32,
            ).reshape(frames, share, width)
            result = wide[0] * packed[2, 0].astype(jnp.float32)
            for g in range(1, frames):
                result = result + wide[g] * packed[2, g].astype(jnp.float32)
            result = result.astype(jnp.bfloat16)
            if d < frames:
                attended[t, f] = result
                back_copy(t, frames - d).start()
            else:
                returned[t, me] = result
        return carry

    def norm_in(t, d):
        sender = lax.rem(me + frames - d, frames)
        pltpu.make_async_remote_copy(
            src_ref=normed.at[t, sender],
            dst_ref=arrived.at[t, sender],
            send_sem=norm_send.at[t, d],
            recv_sem=norm_recv.at[t, d],
            device_id={"frames": sender},
            device_id_type=MESH,
        ).wait_recv()

    lax.fori_loop(0, tiles, temporal_tile, 0)

    for t in range(tiles):
        for d in range(frames):
            owner = lax.rem(me + frames - d, frames)
            if d:
                pltpu.make_async_remote_copy(
                    src_ref=attended.at[t, owner],
                    dst_ref=returned.at[t, owner],
                    send_sem=back_send.at[t, d],
                    recv_sem=back_recv.at[t, d],
                    device_id={"frames": owner},
                    device_id_type=MESH,
                ).wait_recv()
            here = pl.ds(pl.multiple_of(owner * share, share), share)
            mixed_ref[0, t, here] = (
                hidden[t, here].astype(jnp.float32) + returned[t, owner].astype(jnp.float32)
            ).astype(jnp.bfloat16)

    for t in range(tiles):
        for d in range(1, frames):
            norm_copy(t, d).wait_send()
            back_copy(t, d).wait_send()

    @pl.when(has_below)
    def _():
        for i in range(2):
            edge(i, 0, at + 1).wait_send()

    @pl.when(has_above)
    def _():
        for i in range(2):
            edge(i, 1, at - 1).wait_send()


def local(
    latent,
    query_rows,
    key_rows,
    value_rows,
    cached_out,
    refreshed,
    band_width,
    out_weight,
    temporal_weight,
):
    frame_count, tiles, rows, width = latent.shape
    assert frame_count == 1
    heads = band_width.shape[0]
    frames = lax.axis_size("frames")
    groups = lax.axis_size("space")
    share = rows // frames
    span = rows + 2 * EDGE
    bf16 = latent.dtype
    anywhere = pl.BlockSpec(memory_space=pl.ANY)
    scalars = pl.BlockSpec(memory_space=pltpu.SMEM)
    dma = pltpu.SemaphoreType.DMA
    exchanged = pltpu.VMEM((tiles, frames, share, width), bf16)
    return pl.pallas_call(
        functools.partial(kernel, frames, groups, heads),
        out_shape=jax.ShapeDtypeStruct(latent.shape, bf16),
        in_specs=[anywhere] * 5 + [scalars] * 2 + [anywhere] * 2,
        out_specs=pl.BlockSpec(memory_space=pltpu.VMEM),
        scratch_shapes=[
            pltpu.VMEM((tiles, rows, width), bf16),
            pltpu.VMEM((tiles, span, width), bf16),
            pltpu.VMEM((tiles, span, width), bf16),
            pltpu.VMEM((tiles, rows, width), bf16),
            pltpu.VMEM((tiles, rows, width), bf16),
            pltpu.VMEM(out_weight.shape, bf16),
            pltpu.VMEM(temporal_weight.shape, bf16),
            pltpu.VMEM((rows, width), bf16),
            pltpu.VMEM((tiles, rows, width), bf16),
            exchanged,
            exchanged,
            pltpu.VMEM((3, frames, share, width), bf16),
            exchanged,
            exchanged,
            pltpu.VMEM((width, LANES), bf16),
            pltpu.VMEM((LANES, width), bf16),
            dma((3 * tiles + 4 * (tiles - 1) + 4,)),
            dma((2, 2)),
            dma((2, 2)),
            dma((tiles, frames)),
            dma((tiles, frames)),
            dma((tiles, frames)),
            dma((tiles, frames)),
        ],
        compiler_params=pltpu.CompilerParams(
            collective_id=0, has_side_effects=True, vmem_limit_bytes=60 * 1024 * 1024
        ),
        cost_estimate=pl.CostEstimate(
            flops=12 * 10**9, bytes_accessed=18 * 10**6, transcendentals=3 * 10**6
        ),
    )(
        latent,
        query_rows,
        key_rows,
        value_rows,
        cached_out,
        refreshed,
        band_width,
        out_weight,
        temporal_weight,
    )


def solution(mesh):
    return jax.shard_map(
        local,
        mesh=mesh,
        in_specs=(
            P("frames", "space", None, None),
            P("frames", "space", None, None),
            P("frames", "space", None, None),
            P("frames", "space", None, None),
            P("frames", "space", None, None),
            P("frames", "space"),
            P(),
            P(),
            P(),
        ),
        out_specs=P("frames", "space", None, None),
        check_vma=False,
    )
```

```python
import functools
import math

import jax
import jax.numpy as jnp
from jax import lax
from jax.experimental import pallas as pl
from jax.experimental.pallas import tpu as pltpu
from jax.sharding import PartitionSpec as P

EDGE = 64
PARTS = 2
LANES = 128
MESH = pl.DeviceIdType.MESH


def kernel(
    frames,
    groups,
    heads,
    latent_hbm,
    query_hbm,
    key_hbm,
    value_hbm,
    cached_hbm,
    refreshed_ref,
    band_ref,
    out_weight_hbm,
    temporal_weight_hbm,
    hidden_out,
    temporal_out,
    query,
    key,
    value,
    latent,
    cached,
    out_weight,
    temporal_weight,
    spatial,
    hidden,
    normed,
    arrived,
    packed,
    attended,
    gather,
    spread,
    load_sem,
    edge_send,
    edge_recv,
    norm_send,
    norm_recv,
    back_send,
    back_recv,
    hidden_sem,
    own_sem,
):
    _, tiles, rows, width = latent_hbm.shape
    share = rows // frames
    part = rows // PARTS
    piece_rows = part // frames
    span = rows + 2 * EDGE
    head_dim = width // heads
    me = lax.axis_index("frames")
    at = lax.axis_index("space")
    chips = frames // 2
    chip, core = me // 2, lax.rem(me, 2)
    steps = [(k, j) for k in range(1, chips) for j in range(2)] + [(0, 1)]

    def target_of(i):
        k, j = steps[i]
        return lax.rem(chip + k, chips) * 2 + lax.rem(core + j, 2)

    def source_of(i):
        k, j = steps[i]
        return lax.rem(chip + chips - k, chips) * 2 + lax.rem(core + j, 2)

    others = range(frames - 1)
    has_above = at > 0
    has_below = at < groups - 1

    barrier = pltpu.get_barrier_semaphore()
    for i in others:
        pl.semaphore_signal(
            barrier, inc=1, device_id={"frames": target_of(i)}, device_id_type=MESH
        )

    @pl.when(has_above)
    def _():
        pl.semaphore_signal(barrier, inc=1, device_id={"space": at - 1}, device_id_type=MESH)

    @pl.when(has_below)
    def _():
        pl.semaphore_signal(barrier, inc=1, device_id={"space": at + 1}, device_id_type=MESH)

    loads = []

    def load(src, dst):
        copy = pltpu.make_async_copy(src, dst, load_sem.at[len(loads)])
        copy.start()
        loads.append(copy)

    for t in range(tiles):
        load(query_hbm.at[0, t], query.at[t])
        for src, dst in ((key_hbm, key), (value_hbm, value)):
            load(src.at[0, t], dst.at[t, pl.ds(EDGE, rows)])
            if t > 0:
                load(src.at[0, t - 1, pl.ds(rows - EDGE, EDGE)], dst.at[t, pl.ds(0, EDGE)])
            if t < tiles - 1:
                load(src.at[0, t + 1, pl.ds(0, EDGE)], dst.at[t, pl.ds(rows + EDGE, EDGE)])

    peers = frames - 1 + jnp.where(has_above, 1, 0) + jnp.where(has_below, 1, 0)
    pl.semaphore_wait(barrier, peers)

    def edge(i, which, target):
        src, dst = ((key_hbm, key), (value_hbm, value))[i]
        if which == 0:
            source = src.at[0, tiles - 1, pl.ds(rows - EDGE, EDGE)]
            place = dst.at[0, pl.ds(0, EDGE)]
        else:
            source = src.at[0, 0, pl.ds(0, EDGE)]
            place = dst.at[tiles - 1, pl.ds(rows + EDGE, EDGE)]
        return pltpu.make_async_remote_copy(
            src_ref=source,
            dst_ref=place,
            send_sem=edge_send.at[which, i],
            recv_sem=edge_recv.at[which, i],
            device_id={"space": target},
            device_id_type=MESH,
        )

    @pl.when(has_below)
    def _():
        for i in range(2):
            edge(i, 0, at + 1).start()

    @pl.when(has_above)
    def _():
        for i in range(2):
            edge(i, 1, at - 1).start()

    load(cached_hbm.at[0], cached)
    load(latent_hbm.at[0], latent)
    load(out_weight_hbm, out_weight)
    early = len(loads)
    load(temporal_weight_hbm, temporal_weight)

    @pl.when(jnp.logical_not(has_above))
    def _():
        for dst in (key, value):
            dst[0, pl.ds(0, EDGE)] = jnp.zeros((EDGE, width), dst.dtype)

    @pl.when(jnp.logical_not(has_below))
    def _():
        for dst in (key, value):
            dst[tiles - 1, pl.ds(rows + EDGE, EDGE)] = jnp.zeros((EDGE, width), dst.dtype)

    column = lax.broadcasted_iota(jnp.int32, (width, LANES), 0)
    first = lax.broadcasted_iota(jnp.int32, (width, LANES), 1) * head_dim
    inside = jnp.where((column >= first) & (column < first + head_dim), 1.0, 0.0)
    gather[...] = inside.astype(jnp.bfloat16)
    column = lax.broadcasted_iota(jnp.int32, (LANES, width), 1)
    first = lax.broadcasted_iota(jnp.int32, (LANES, width), 0) * head_dim
    inside = jnp.where((column >= first) & (column < first + head_dim), 1.0, 0.0)
    spread[...] = inside.astype(jnp.bfloat16)
    lane = lax.broadcasted_iota(jnp.int32, (1, LANES), 1)
    band = jnp.zeros((1, LANES), jnp.int32)
    for h in range(heads):
        band = jnp.where(lane == h, band_ref[h], band)

    for copy in loads[:early]:
        copy.wait()

    @pl.when(has_above)
    def _():
        for i in range(2):
            edge(i, 0, at - 1).wait_recv()

    @pl.when(has_below)
    def _():
        for i in range(2):
            edge(i, 1, at + 1).wait_recv()

    scale = math.log2(math.e) / math.sqrt(head_dim)
    position = lax.broadcasted_iota(jnp.int32, (1, span), 1)

    def norm_copy(t, c, i, peer):
        return pltpu.make_async_remote_copy(
            src_ref=normed.at[t, c, peer],
            dst_ref=arrived.at[t, me, c],
            send_sem=norm_send.at[t, c, i],
            recv_sem=norm_recv.at[t, c, i],
            device_id={"frames": peer},
            device_id_type=MESH,
        )

    def norm_in(t, c, i):
        sender = source_of(i)
        return pltpu.make_async_remote_copy(
            src_ref=normed.at[t, c, sender],
            dst_ref=arrived.at[t, sender, c],
            send_sem=norm_send.at[t, c, i],
            recv_sem=norm_recv.at[t, c, i],
            device_id={"frames": sender},
            device_id_type=MESH,
        )

    def back_copy(t, i, peer):
        return pltpu.make_async_remote_copy(
            src_ref=attended.at[t, peer],
            dst_ref=temporal_out.at[0, t, :, me],
            send_sem=back_send.at[t, i],
            recv_sem=back_recv.at[t, i],
            device_id={"frames": peer},
            device_id_type=MESH,
        )

    def back_in(t, i):
        owner = source_of(i)
        return pltpu.make_async_remote_copy(
            src_ref=attended.at[t, owner],
            dst_ref=temporal_out.at[0, t, :, owner],
            send_sem=back_send.at[t, i],
            recv_sem=back_recv.at[t, i],
            device_id={"frames": owner},
            device_id_type=MESH,
        )

    def own_copy(t):
        return pltpu.make_async_copy(
            attended.at[t, me], temporal_out.at[0, t, :, me], own_sem.at[t]
        )

    def hidden_copy(t, c):
        return pltpu.make_async_copy(
            hidden.at[t, c], hidden_out.at[0, t, c], hidden_sem.at[t, c]
        )

    def head_blocks(h):
        start, stop = h * head_dim, (h + 1) * head_dim
        return start, stop, start // LANES, -(-stop // LANES)

    def spatial_part(n, carry):
        t, c = n // PARTS, lax.rem(n, PARTS)
        here = pl.ds(pl.multiple_of(c * part, part), part)
        whole = at * tiles + t
        low = jnp.where(whole == 0, EDGE, 0)
        high = jnp.where(whole == groups * tiles - 1, rows + EDGE, span)
        bias = jnp.where((position >= low) & (position < high), 0.0, -jnp.inf)
        fresh_here = refreshed_ref[0, t] == 1

        def scores_of(h):
            start, stop, a, b = head_blocks(h)
            cols = slice(a * LANES, b * LANES)
            at_col = lax.broadcasted_iota(jnp.int32, (1, (b - a) * LANES), 1) + a * LANES
            mine = (at_col >= start) & (at_col < stop)
            q = query[t, here, cols] * jnp.where(mine, 1.0, 0.0).astype(jnp.bfloat16)
            return lax.dot_general(
                q, key[t, :, cols], (((1,), (1,)), ((), ())), preferred_element_type=jnp.float32
            )

        partial = None
        ahead = scores_of(0)
        for h in range(heads):
            start, stop, a, b = head_blocks(h)
            scores = ahead + bias
            if h < heads - 1:
                ahead = scores_of(h + 1)
            top = jnp.max(scores, axis=-1, keepdims=True)
            expo = jnp.exp2((scores - top) * scale)
            total = jnp.sum(expo, axis=-1, keepdims=True)
            out = jnp.dot(
                expo.astype(jnp.bfloat16),
                value[t, :, a * LANES : b * LANES],
                preferred_element_type=jnp.float32,
            )
            out = out * (1.0 / total)
            for block in range(a, b):
                piece = out[:, (block - a) * LANES : (block - a + 1) * LANES]
                if start > block * LANES:
                    piece = jnp.where(lane + block * LANES >= start, piece, partial)
                if stop >= (block + 1) * LANES:
                    old = cached[t, here, block * LANES : (block + 1) * LANES]
                    spatial[:, block * LANES : (block + 1) * LANES] = jnp.where(
                        fresh_here, piece.astype(jnp.bfloat16), old
                    )
                else:
                    partial = piece
        projected = jnp.dot(spatial[...], out_weight[...], preferred_element_type=jnp.float32)
        hid = (latent[t, here].astype(jnp.float32) + projected).astype(jnp.bfloat16)
        hidden[t, c] = hid.reshape(frames, piece_rows, width)
        hid32 = hid.astype(jnp.float32)
        mean = jnp.mean(hid32 * hid32, axis=-1, keepdims=True)
        norm = (hid32 * lax.rsqrt(mean + 1e-06)).astype(jnp.bfloat16)
        normed[t, c] = norm.reshape(frames, piece_rows, width)
        for i in others:
            norm_copy(t, c, i, target_of(i)).start()
        hidden_copy(t, c).start()
        arrived[t, me, c] = normed[t, c, me]
        return carry

    lax.fori_loop(0, tiles * PARTS, spatial_part, 0)
    loads[early].wait()

    def temporal_tile(t, carry):
        for c in range(PARTS):
            for i in others:
                norm_in(t, c, i).wait_recv()
        block = arrived[t].reshape(frames * share, width)

        def project(j, c):
            w = temporal_weight[:, pl.ds(pl.multiple_of(j * width, LANES), width)]
            flat = jnp.dot(block, w, preferred_element_type=jnp.float32).astype(jnp.bfloat16)
            packed[j] = flat.reshape(frames, share, width)
            return c

        lax.fori_loop(0, 3, project, 0)
        for i in range(frames):
            f = target_of(i) if i < frames - 1 else me
            products = packed[0, f][None] * packed[1]
            scores = jnp.dot(
                products.reshape(frames * share, width),
                gather[...],
                preferred_element_type=jnp.float32,
            ).reshape(frames, share, LANES)
            scores = [
                jnp.where(jnp.abs(f - g) <= band, scores[g], -jnp.inf) for g in range(frames)
            ]
            top = functools.reduce(jnp.maximum, scores)
            expo = [jnp.exp2((s - top) * scale) for s in scores]
            inverse = 1.0 / functools.reduce(jnp.add, expo)
            weights = jnp.stack([(e * inverse).astype(jnp.bfloat16) for e in expo])
            wide = jnp.dot(
                weights.reshape(frames * share, LANES),
                spread[...],
                preferred_element_type=jnp.float32,
            ).reshape(frames, share, width)
            result = wide[0] * packed[2, 0].astype(jnp.float32)
            for g in range(1, frames):
                result = result + wide[g] * packed[2, g].astype(jnp.float32)
            attended[t, f] = result.astype(jnp.bfloat16).reshape(PARTS, piece_rows, width)
            if i < frames - 1:
                back_copy(t, i, f).start()
            else:
                own_copy(t).start()
        return carry

    lax.fori_loop(0, tiles, temporal_tile, 0)

    for t in range(tiles):
        for c in range(PARTS):
            hidden_copy(t, c).wait()
            for i in others:
                norm_copy(t, c, i, target_of(i)).wait_send()
        own_copy(t).wait()
        for i in others:
            back_copy(t, i, target_of(i)).wait_send()
            back_in(t, i).wait_recv()

    @pl.when(has_below)
    def _():
        for i in range(2):
            edge(i, 0, at + 1).wait_send()

    @pl.when(has_above)
    def _():
        for i in range(2):
            edge(i, 1, at - 1).wait_send()


def local(
    latent,
    query_rows,
    key_rows,
    value_rows,
    cached_out,
    refreshed,
    band_width,
    out_weight,
    temporal_weight,
):
    frame_count, tiles, rows, width = latent.shape
    assert frame_count == 1
    heads = band_width.shape[0]
    frames = lax.axis_size("frames")
    groups = lax.axis_size("space")
    share = rows // frames
    span = rows + 2 * EDGE
    bf16 = latent.dtype
    anywhere = pl.BlockSpec(memory_space=pl.ANY)
    scalars = pl.BlockSpec(memory_space=pltpu.SMEM)
    dma = pltpu.SemaphoreType.DMA
    piece = share // PARTS
    shape = (1, tiles, PARTS, frames, piece, width)
    hidden, temporal = pl.pallas_call(
        functools.partial(kernel, frames, groups, heads),
        out_shape=[jax.ShapeDtypeStruct(shape, bf16)] * 2,
        in_specs=[anywhere] * 5 + [scalars] * 2 + [anywhere] * 2,
        out_specs=[anywhere] * 2,
        scratch_shapes=[
            pltpu.VMEM((tiles, rows, width), bf16),
            pltpu.VMEM((tiles, span, width), bf16),
            pltpu.VMEM((tiles, span, width), bf16),
            pltpu.VMEM((tiles, rows, width), bf16),
            pltpu.VMEM((tiles, rows, width), bf16),
            pltpu.VMEM(out_weight.shape, bf16),
            pltpu.VMEM(temporal_weight.shape, bf16),
            pltpu.VMEM((rows // PARTS, width), bf16),
            pltpu.VMEM(shape[1:], bf16),
            pltpu.VMEM(shape[1:], bf16),
            pltpu.VMEM((tiles, frames, PARTS, piece, width), bf16),
            pltpu.VMEM((3, frames, share, width), bf16),
            pltpu.VMEM((tiles, frames, PARTS, piece, width), bf16),
            pltpu.VMEM((width, LANES), bf16),
            pltpu.VMEM((LANES, width), bf16),
            dma((3 * tiles + 4 * (tiles - 1) + 4,)),
            dma((2, 2)),
            dma((2, 2)),
            dma((tiles, PARTS, frames - 1)),
            dma((tiles, PARTS, frames - 1)),
            dma((tiles, frames - 1)),
            dma((tiles, frames - 1)),
            dma((tiles, PARTS)),
            dma((tiles,)),
        ],
        compiler_params=pltpu.CompilerParams(
            collective_id=0, has_side_effects=True, vmem_limit_bytes=60 * 1024 * 1024
        ),
        cost_estimate=pl.CostEstimate(
            flops=12 * 10**9, bytes_accessed=18 * 10**6, transcendentals=3 * 10**6
        ),
    )(
        latent,
        query_rows,
        key_rows,
        value_rows,
        cached_out,
        refreshed,
        band_width,
        out_weight,
        temporal_weight,
    )
    mixed = hidden.astype(jnp.float32) + temporal.astype(jnp.float32)
    return mixed.astype(jnp.bfloat16).reshape(latent.shape)


def solution(mesh):
    return jax.shard_map(
        local,
        mesh=mesh,
        in_specs=(
            P("frames", "space", None, None),
            P("frames", "space", None, None),
            P("frames", "space", None, None),
            P("frames", "space", None, None),
            P("frames", "space", None, None),
            P("frames", "space"),
            P(),
            P(),
            P(),
        ),
        out_specs=P("frames", "space", None, None),
        check_vma=False,
    )
```

```python
import functools
import math

import jax
import jax.numpy as jnp
from jax import lax
from jax.experimental import pallas as pl
from jax.experimental.pallas import tpu as pltpu
from jax.sharding import PartitionSpec as P

EDGE = 64
PARTS = 2
LANES = 128
MESH = pl.DeviceIdType.MESH


def kernel(
    frames,
    groups,
    heads,
    latent_hbm,
    query_hbm,
    key_hbm,
    value_hbm,
    cached_hbm,
    refreshed_ref,
    band_ref,
    out_weight_hbm,
    temporal_weight_hbm,
    hidden_out,
    temporal_out,
    query,
    key,
    value,
    latent,
    cached,
    out_weight,
    temporal_weight,
    spatial,
    hidden,
    normed,
    arrived,
    packed,
    attended,
    gather,
    spread,
    load_sem,
    edge_send,
    edge_recv,
    norm_send,
    norm_recv,
    back_send,
    back_recv,
    hidden_sem,
    own_sem,
):
    _, tiles, rows, width = latent_hbm.shape
    share = rows // frames
    part = rows // PARTS
    piece_rows = part // frames
    span = rows + 2 * EDGE
    head_dim = width // heads
    me = lax.axis_index("frames")
    at = lax.axis_index("space")
    chips = frames // 2
    chip, core = me // 2, lax.rem(me, 2)
    steps = [(k, j) for k in range(1, chips) for j in range(2)] + [(0, 1)]

    def target_of(i):
        k, j = steps[i]
        return lax.rem(chip + k, chips) * 2 + lax.rem(core + j, 2)

    def source_of(i):
        k, j = steps[i]
        return lax.rem(chip + chips - k, chips) * 2 + lax.rem(core + j, 2)

    others = range(frames - 1)
    has_above = at > 0
    has_below = at < groups - 1

    barrier = pltpu.get_barrier_semaphore()
    for i in others:
        pl.semaphore_signal(
            barrier, inc=1, device_id={"frames": target_of(i)}, device_id_type=MESH
        )

    @pl.when(has_above)
    def _():
        pl.semaphore_signal(barrier, inc=1, device_id={"space": at - 1}, device_id_type=MESH)

    @pl.when(has_below)
    def _():
        pl.semaphore_signal(barrier, inc=1, device_id={"space": at + 1}, device_id_type=MESH)

    loads = []

    def load(src, dst):
        copy = pltpu.make_async_copy(src, dst, load_sem.at[len(loads)])
        copy.start()
        loads.append(copy)

    for t in range(tiles):
        load(query_hbm.at[0, t], query.at[t])
        for src, dst in ((key_hbm, key), (value_hbm, value)):
            load(src.at[0, t], dst.at[t, pl.ds(EDGE, rows)])
            if t > 0:
                load(src.at[0, t - 1, pl.ds(rows - EDGE, EDGE)], dst.at[t, pl.ds(0, EDGE)])
            if t < tiles - 1:
                load(src.at[0, t + 1, pl.ds(0, EDGE)], dst.at[t, pl.ds(rows + EDGE, EDGE)])

    peers = frames - 1 + jnp.where(has_above, 1, 0) + jnp.where(has_below, 1, 0)
    pl.semaphore_wait(barrier, peers)

    def edge(i, which, target):
        src, dst = ((key_hbm, key), (value_hbm, value))[i]
        if which == 0:
            source = src.at[0, tiles - 1, pl.ds(rows - EDGE, EDGE)]
            place = dst.at[0, pl.ds(0, EDGE)]
        else:
            source = src.at[0, 0, pl.ds(0, EDGE)]
            place = dst.at[tiles - 1, pl.ds(rows + EDGE, EDGE)]
        return pltpu.make_async_remote_copy(
            src_ref=source,
            dst_ref=place,
            send_sem=edge_send.at[which, i],
            recv_sem=edge_recv.at[which, i],
            device_id={"space": target},
            device_id_type=MESH,
        )

    @pl.when(has_below)
    def _():
        for i in range(2):
            edge(i, 0, at + 1).start()

    load(cached_hbm.at[0], cached)
    load(latent_hbm.at[0], latent)
    load(out_weight_hbm, out_weight)
    early = len(loads)
    load(temporal_weight_hbm, temporal_weight)

    @pl.when(jnp.logical_not(has_above))
    def _():
        for dst in (key, value):
            dst[0, pl.ds(0, EDGE)] = jnp.zeros((EDGE, width), dst.dtype)

    @pl.when(jnp.logical_not(has_below))
    def _():
        for dst in (key, value):
            dst[tiles - 1, pl.ds(rows + EDGE, EDGE)] = jnp.zeros((EDGE, width), dst.dtype)

    column = lax.broadcasted_iota(jnp.int32, (width, LANES), 0)
    first = lax.broadcasted_iota(jnp.int32, (width, LANES), 1) * head_dim
    inside = jnp.where((column >= first) & (column < first + head_dim), 1.0, 0.0)
    gather[...] = inside.astype(jnp.bfloat16)
    column = lax.broadcasted_iota(jnp.int32, (LANES, width), 1)
    first = lax.broadcasted_iota(jnp.int32, (LANES, width), 0) * head_dim
    inside = jnp.where((column >= first) & (column < first + head_dim), 1.0, 0.0)
    spread[...] = inside.astype(jnp.bfloat16)
    lane = lax.broadcasted_iota(jnp.int32, (1, LANES), 1)
    band = jnp.zeros((1, LANES), jnp.int32)
    for h in range(heads):
        band = jnp.where(lane == h, band_ref[h], band)

    for copy in loads[:early]:
        copy.wait()

    @pl.when(has_above)
    def _():
        for i in range(2):
            edge(i, 0, at - 1).wait_recv()

    @pl.when(has_below)
    def _():
        for i in range(2):
            edge(i, 0, at + 1).wait_send()

    @pl.when(has_above)
    def _():
        for i in range(2):
            edge(i, 1, at - 1).start()

    scale = math.log2(math.e) / math.sqrt(head_dim)
    position = lax.broadcasted_iota(jnp.int32, (1, span), 1)

    def norm_copy(t, c, i, peer):
        return pltpu.make_async_remote_copy(
            src_ref=normed.at[t, c, peer],
            dst_ref=arrived.at[t, me, c],
            send_sem=norm_send.at[t, c, i],
            recv_sem=norm_recv.at[t, c, i],
            device_id={"frames": peer},
            device_id_type=MESH,
        )

    def norm_in(t, c, i):
        sender = source_of(i)
        return pltpu.make_async_remote_copy(
            src_ref=normed.at[t, c, sender],
            dst_ref=arrived.at[t, sender, c],
            send_sem=norm_send.at[t, c, i],
            recv_sem=norm_recv.at[t, c, i],
            device_id={"frames": sender},
            device_id_type=MESH,
        )

    def back_copy(t, i, peer):
        return pltpu.make_async_remote_copy(
            src_ref=attended.at[t, peer],
            dst_ref=temporal_out.at[0, t, :, me],
            send_sem=back_send.at[t, i],
            recv_sem=back_recv.at[t, i],
            device_id={"frames": peer},
            device_id_type=MESH,
        )

    def back_in(t, i):
        owner = source_of(i)
        return pltpu.make_async_remote_copy(
            src_ref=attended.at[t, owner],
            dst_ref=temporal_out.at[0, t, :, owner],
            send_sem=back_send.at[t, i],
            recv_sem=back_recv.at[t, i],
            device_id={"frames": owner},
            device_id_type=MESH,
        )

    def own_copy(t):
        return pltpu.make_async_copy(
            attended.at[t, me], temporal_out.at[0, t, :, me], own_sem.at[t]
        )

    def hidden_copy(t, c):
        return pltpu.make_async_copy(
            hidden.at[t, c], hidden_out.at[0, t, c], hidden_sem.at[t, c]
        )

    def head_blocks(h):
        start, stop = h * head_dim, (h + 1) * head_dim
        return start, stop, start // LANES, -(-stop // LANES)

    def spatial_part(n, carry):
        t, c = n // PARTS, lax.rem(n, PARTS)

        @pl.when(jnp.logical_and(has_below, n == (tiles - 1) * PARTS))
        def _():
            for i in range(2):
                edge(i, 1, at + 1).wait_recv()

        here = pl.ds(pl.multiple_of(c * part, part), part)
        whole = at * tiles + t
        low = jnp.where(whole == 0, EDGE, 0)
        high = jnp.where(whole == groups * tiles - 1, rows + EDGE, span)
        bias = jnp.where((position >= low) & (position < high), 0.0, -jnp.inf)
        fresh_here = refreshed_ref[0, t] == 1

        def scores_of(h):
            start, stop, a, b = head_blocks(h)
            cols = slice(a * LANES, b * LANES)
            at_col = lax.broadcasted_iota(jnp.int32, (1, (b - a) * LANES), 1) + a * LANES
            mine = (at_col >= start) & (at_col < stop)
            q = query[t, here, cols] * jnp.where(mine, 1.0, 0.0).astype(jnp.bfloat16)
            return lax.dot_general(
                q, key[t, :, cols], (((1,), (1,)), ((), ())), preferred_element_type=jnp.float32
            )

        partial = None
        ahead = scores_of(0)
        for h in range(heads):
            start, stop, a, b = head_blocks(h)
            scores = ahead + bias
            if h < heads - 1:
                ahead = scores_of(h + 1)
            top = jnp.max(scores, axis=-1, keepdims=True)
            expo = jnp.exp2((scores - top) * scale)
            total = jnp.sum(expo, axis=-1, keepdims=True)
            out = jnp.dot(
                expo.astype(jnp.bfloat16),
                value[t, :, a * LANES : b * LANES],
                preferred_element_type=jnp.float32,
            )
            out = out * (1.0 / total)
            for block in range(a, b):
                piece = out[:, (block - a) * LANES : (block - a + 1) * LANES]
                if start > block * LANES:
                    piece = jnp.where(lane + block * LANES >= start, piece, partial)
                if stop >= (block + 1) * LANES:
                    old = cached[t, here, block * LANES : (block + 1) * LANES]
                    spatial[:, block * LANES : (block + 1) * LANES] = jnp.where(
                        fresh_here, piece.astype(jnp.bfloat16), old
                    )
                else:
                    partial = piece
        projected = jnp.dot(spatial[...], out_weight[...], preferred_element_type=jnp.float32)
        hid = (latent[t, here].astype(jnp.float32) + projected).astype(jnp.bfloat16)
        hidden[t, c] = hid.reshape(frames, piece_rows, width)
        hid32 = hid.astype(jnp.float32)
        mean = jnp.mean(hid32 * hid32, axis=-1, keepdims=True)
        norm = (hid32 * lax.rsqrt(mean + 1e-06)).astype(jnp.bfloat16)
        normed[t, c] = norm.reshape(frames, piece_rows, width)
        for i in others:
            norm_copy(t, c, i, target_of(i)).start()
        hidden_copy(t, c).start()
        arrived[t, me, c] = normed[t, c, me]
        return carry

    lax.fori_loop(0, tiles * PARTS, spatial_part, 0)
    loads[early].wait()

    def temporal_tile(t, carry):
        for c in range(PARTS):
            for i in others:
                norm_in(t, c, i).wait_recv()
        block = arrived[t].reshape(frames * share, width)

        def project(j, c):
            w = temporal_weight[:, pl.ds(pl.multiple_of(j * width, LANES), width)]
            flat = jnp.dot(block, w, preferred_element_type=jnp.float32).astype(jnp.bfloat16)
            packed[j] = flat.reshape(frames, share, width)
            return c

        lax.fori_loop(0, 3, project, 0)
        for i in range(frames):
            f = target_of(i) if i < frames - 1 else me
            products = packed[0, f][None] * packed[1]
            scores = jnp.dot(
                products.reshape(frames * share, width),
                gather[...],
                preferred_element_type=jnp.float32,
            ).reshape(frames, share, LANES)
            scores = [
                jnp.where(jnp.abs(f - g) <= band, scores[g], -jnp.inf) for g in range(frames)
            ]
            top = functools.reduce(jnp.maximum, scores)
            expo = [jnp.exp2((s - top) * scale) for s in scores]
            inverse = 1.0 / functools.reduce(jnp.add, expo)
            weights = jnp.stack([(e * inverse).astype(jnp.bfloat16) for e in expo])
            wide = jnp.dot(
                weights.reshape(frames * share, LANES),
                spread[...],
                preferred_element_type=jnp.float32,
            ).reshape(frames, share, width)
            result = wide[0] * packed[2, 0].astype(jnp.float32)
            for g in range(1, frames):
                result = result + wide[g] * packed[2, g].astype(jnp.float32)
            attended[t, f] = result.astype(jnp.bfloat16).reshape(PARTS, piece_rows, width)
            if i < frames - 1:
                back_copy(t, i, f).start()
            else:
                own_copy(t).start()
        return carry

    lax.fori_loop(0, tiles, temporal_tile, 0)

    for t in range(tiles):
        for c in range(PARTS):
            hidden_copy(t, c).wait()
            for i in others:
                norm_copy(t, c, i, target_of(i)).wait_send()
        own_copy(t).wait()
        for i in others:
            back_copy(t, i, target_of(i)).wait_send()
            back_in(t, i).wait_recv()

    @pl.when(has_above)
    def _():
        for i in range(2):
            edge(i, 1, at - 1).wait_send()


def add_kernel(hidden_ref, temporal_ref, mixed_ref):
    total = hidden_ref[...].astype(jnp.float32) + temporal_ref[...].astype(jnp.float32)
    mixed_ref[...] = total.astype(jnp.bfloat16)


def local(
    latent,
    query_rows,
    key_rows,
    value_rows,
    cached_out,
    refreshed,
    band_width,
    out_weight,
    temporal_weight,
):
    frame_count, tiles, rows, width = latent.shape
    assert frame_count == 1
    heads = band_width.shape[0]
    frames = lax.axis_size("frames")
    groups = lax.axis_size("space")
    share = rows // frames
    span = rows + 2 * EDGE
    bf16 = latent.dtype
    anywhere = pl.BlockSpec(memory_space=pl.ANY)
    scalars = pl.BlockSpec(memory_space=pltpu.SMEM)
    dma = pltpu.SemaphoreType.DMA
    piece = share // PARTS
    shape = (1, tiles, PARTS, frames, piece, width)
    hidden, temporal = pl.pallas_call(
        functools.partial(kernel, frames, groups, heads),
        out_shape=[jax.ShapeDtypeStruct(shape, bf16)] * 2,
        in_specs=[anywhere] * 5 + [scalars] * 2 + [anywhere] * 2,
        out_specs=[anywhere] * 2,
        scratch_shapes=[
            pltpu.VMEM((tiles, rows, width), bf16),
            pltpu.VMEM((tiles, span, width), bf16),
            pltpu.VMEM((tiles, span, width), bf16),
            pltpu.VMEM((tiles, rows, width), bf16),
            pltpu.VMEM((tiles, rows, width), bf16),
            pltpu.VMEM(out_weight.shape, bf16),
            pltpu.VMEM(temporal_weight.shape, bf16),
            pltpu.VMEM((rows // PARTS, width), bf16),
            pltpu.VMEM(shape[1:], bf16),
            pltpu.VMEM(shape[1:], bf16),
            pltpu.VMEM((tiles, frames, PARTS, piece, width), bf16),
            pltpu.VMEM((3, frames, share, width), bf16),
            pltpu.VMEM((tiles, frames, PARTS, piece, width), bf16),
            pltpu.VMEM((width, LANES), bf16),
            pltpu.VMEM((LANES, width), bf16),
            dma((3 * tiles + 4 * (tiles - 1) + 4,)),
            dma((2, 2)),
            dma((2, 2)),
            dma((tiles, PARTS, frames - 1)),
            dma((tiles, PARTS, frames - 1)),
            dma((tiles, frames - 1)),
            dma((tiles, frames - 1)),
            dma((tiles, PARTS)),
            dma((tiles,)),
        ],
        compiler_params=pltpu.CompilerParams(
            collective_id=0, has_side_effects=True, vmem_limit_bytes=60 * 1024 * 1024
        ),
        cost_estimate=pl.CostEstimate(
            flops=12 * 10**9, bytes_accessed=18 * 10**6, transcendentals=3 * 10**6
        ),
    )(
        latent,
        query_rows,
        key_rows,
        value_rows,
        cached_out,
        refreshed,
        band_width,
        out_weight,
        temporal_weight,
    )
    block = pl.BlockSpec((rows // PARTS, width), lambda i: (i, 0))
    flat = (tiles * rows, width)
    mixed = pl.pallas_call(
        add_kernel,
        out_shape=jax.ShapeDtypeStruct(flat, bf16),
        grid=(tiles * PARTS,),
        in_specs=[block, block],
        out_specs=block,
    )(hidden.reshape(flat), temporal.reshape(flat))
    return mixed.reshape(latent.shape)


def solution(mesh):
    return jax.shard_map(
        local,
        mesh=mesh,
        in_specs=(
            P("frames", "space", None, None),
            P("frames", "space", None, None),
            P("frames", "space", None, None),
            P("frames", "space", None, None),
            P("frames", "space", None, None),
            P("frames", "space"),
            P(),
            P(),
            P(),
        ),
        out_specs=P("frames", "space", None, None),
        check_vma=False,
    )
```

```python
import functools
import math

import jax
import jax.numpy as jnp
from jax import lax
from jax.experimental import pallas as pl
from jax.experimental.pallas import tpu as pltpu
from jax.sharding import PartitionSpec as P

EDGE = 64
PARTS = 2
LANES = 128
MESH = pl.DeviceIdType.MESH


def kernel(
    frames,
    groups,
    heads,
    latent_hbm,
    query_hbm,
    key_hbm,
    value_hbm,
    cached_hbm,
    refreshed_ref,
    band_ref,
    out_weight_hbm,
    temporal_weight_hbm,
    hidden_out,
    temporal_out,
    query,
    key,
    value,
    latent,
    cached,
    out_weight,
    temporal_weight,
    spatial,
    hidden,
    normed,
    arrived,
    packed,
    attended,
    gather,
    spread,
    tops,
    totals,
    unscaled,
    load_sem,
    edge_send,
    edge_recv,
    norm_send,
    norm_recv,
    back_send,
    back_recv,
    hidden_sem,
    own_sem,
):
    _, tiles, rows, width = latent_hbm.shape
    share = rows // frames
    part = rows // PARTS
    piece_rows = part // frames
    head_dim = width // heads
    me = lax.axis_index("frames")
    at = lax.axis_index("space")
    chips = frames // 2
    chip, core = me // 2, lax.rem(me, 2)
    steps = [(k, j) for k in range(1, chips) for j in range(2)] + [(0, 1)]

    def target_of(i):
        k, j = steps[i]
        return lax.rem(chip + k, chips) * 2 + lax.rem(core + j, 2)

    def source_of(i):
        k, j = steps[i]
        return lax.rem(chip + chips - k, chips) * 2 + lax.rem(core + j, 2)

    others = range(frames - 1)
    has_above = at > 0
    has_below = at < groups - 1

    barrier = pltpu.get_barrier_semaphore()
    for i in others:
        pl.semaphore_signal(
            barrier, inc=1, device_id={"frames": target_of(i)}, device_id_type=MESH
        )

    @pl.when(has_above)
    def _():
        pl.semaphore_signal(barrier, inc=1, device_id={"space": at - 1}, device_id_type=MESH)

    @pl.when(has_below)
    def _():
        pl.semaphore_signal(barrier, inc=1, device_id={"space": at + 1}, device_id_type=MESH)

    loads = []

    def load(src, dst):
        copy = pltpu.make_async_copy(src, dst, load_sem.at[len(loads)])
        copy.start()
        loads.append(copy)

    for t in range(tiles):
        load(query_hbm.at[0, t], query.at[t])
        for src, dst in ((key_hbm, key), (value_hbm, value)):
            load(src.at[0, t], dst.at[t, pl.ds(EDGE, rows)])
            if t > 0:
                load(src.at[0, t - 1, pl.ds(rows - EDGE, EDGE)], dst.at[t, pl.ds(0, EDGE)])
            if t < tiles - 1:
                load(src.at[0, t + 1, pl.ds(0, EDGE)], dst.at[t, pl.ds(rows + EDGE, EDGE)])

    peers = frames - 1 + jnp.where(has_above, 1, 0) + jnp.where(has_below, 1, 0)
    pl.semaphore_wait(barrier, peers)

    def edge(i, which, target):
        src, dst = ((key_hbm, key), (value_hbm, value))[i]
        if which == 0:
            source = src.at[0, tiles - 1, pl.ds(rows - EDGE, EDGE)]
            place = dst.at[0, pl.ds(0, EDGE)]
        else:
            source = src.at[0, 0, pl.ds(0, EDGE)]
            place = dst.at[tiles - 1, pl.ds(rows + EDGE, EDGE)]
        return pltpu.make_async_remote_copy(
            src_ref=source,
            dst_ref=place,
            send_sem=edge_send.at[which, i],
            recv_sem=edge_recv.at[which, i],
            device_id={"space": target},
            device_id_type=MESH,
        )

    @pl.when(has_below)
    def _():
        for i in range(2):
            edge(i, 0, at + 1).start()

    ready = len(loads)
    load(cached_hbm.at[0], cached)
    load(latent_hbm.at[0], latent)
    load(out_weight_hbm, out_weight)
    early = len(loads)
    load(temporal_weight_hbm, temporal_weight)

    @pl.when(jnp.logical_not(has_above))
    def _():
        for dst in (key, value):
            dst[0, pl.ds(0, EDGE)] = jnp.zeros((EDGE, width), dst.dtype)

    @pl.when(jnp.logical_not(has_below))
    def _():
        for dst in (key, value):
            dst[tiles - 1, pl.ds(rows + EDGE, EDGE)] = jnp.zeros((EDGE, width), dst.dtype)

    column = lax.broadcasted_iota(jnp.int32, (width, LANES), 0)
    first = lax.broadcasted_iota(jnp.int32, (width, LANES), 1) * head_dim
    inside = jnp.where((column >= first) & (column < first + head_dim), 1.0, 0.0)
    gather[...] = inside.astype(jnp.bfloat16)
    column = lax.broadcasted_iota(jnp.int32, (LANES, width), 1)
    first = lax.broadcasted_iota(jnp.int32, (LANES, width), 0) * head_dim
    inside = jnp.where((column >= first) & (column < first + head_dim), 1.0, 0.0)
    spread[...] = inside.astype(jnp.bfloat16)
    lane = lax.broadcasted_iota(jnp.int32, (1, LANES), 1)
    band = jnp.zeros((1, LANES), jnp.int32)
    for h in range(heads):
        band = jnp.where(lane == h, band_ref[h], band)

    for copy in loads[:ready]:
        copy.wait()


    scale = math.log2(math.e) / math.sqrt(head_dim)

    def norm_copy(t, c, i, peer):
        return pltpu.make_async_remote_copy(
            src_ref=normed.at[t, c, peer],
            dst_ref=arrived.at[t, me, c],
            send_sem=norm_send.at[t, c, i],
            recv_sem=norm_recv.at[t, c, i],
            device_id={"frames": peer},
            device_id_type=MESH,
        )

    def norm_in(t, c, i):
        sender = source_of(i)
        return pltpu.make_async_remote_copy(
            src_ref=normed.at[t, c, sender],
            dst_ref=arrived.at[t, sender, c],
            send_sem=norm_send.at[t, c, i],
            recv_sem=norm_recv.at[t, c, i],
            device_id={"frames": sender},
            device_id_type=MESH,
        )

    def back_copy(t, i, peer):
        return pltpu.make_async_remote_copy(
            src_ref=attended.at[t, peer],
            dst_ref=temporal_out.at[0, t, :, me],
            send_sem=back_send.at[t, i],
            recv_sem=back_recv.at[t, i],
            device_id={"frames": peer},
            device_id_type=MESH,
        )

    def back_in(t, i):
        owner = source_of(i)
        return pltpu.make_async_remote_copy(
            src_ref=attended.at[t, owner],
            dst_ref=temporal_out.at[0, t, :, owner],
            send_sem=back_send.at[t, i],
            recv_sem=back_recv.at[t, i],
            device_id={"frames": owner},
            device_id_type=MESH,
        )

    def own_copy(t):
        return pltpu.make_async_copy(
            attended.at[t, me], temporal_out.at[0, t, :, me], own_sem.at[t]
        )

    def hidden_copy(t, c):
        return pltpu.make_async_copy(
            hidden.at[t, c], hidden_out.at[0, t, c], hidden_sem.at[t, c]
        )

    def head_blocks(h):
        start, stop = h * head_dim, (h + 1) * head_dim
        return start, stop, start // LANES, -(-stop // LANES)

    def scores_of(h, t, here, keys):
        start, stop, a, b = head_blocks(h)
        cols = slice(a * LANES, b * LANES)
        at_col = lax.broadcasted_iota(jnp.int32, (1, (b - a) * LANES), 1) + a * LANES
        mine = (at_col >= start) & (at_col < stop)
        q = query[t, here, cols] * jnp.where(mine, 1.0, 0.0).astype(jnp.bfloat16)
        return lax.dot_general(
            q, key[t, keys, cols], (((1,), (1,)), ((), ())), preferred_element_type=jnp.float32
        )

    def own_keys(t, c):
        here = pl.ds(pl.multiple_of(c * part, part), part)
        keys = pl.ds(pl.multiple_of(jnp.where(t == 0, EDGE, 0), EDGE), rows + EDGE)
        partial = None
        ahead = scores_of(0, t, here, keys)
        for h in range(heads):
            start, stop, a, b = head_blocks(h)
            scores = ahead
            if h < heads - 1:
                ahead = scores_of(h + 1, t, here, keys)
            top = jnp.max(scores, axis=-1, keepdims=True)
            expo = jnp.exp2((scores - top) * scale)
            tops[c, h] = top
            totals[c, h] = jnp.sum(expo, axis=-1, keepdims=True)
            out = jnp.dot(
                expo.astype(jnp.bfloat16),
                value[t, keys, a * LANES : b * LANES],
                preferred_element_type=jnp.float32,
            )
            for block in range(a, b):
                piece = out[:, (block - a) * LANES : (block - a + 1) * LANES]
                if start > block * LANES:
                    piece = jnp.where(lane + block * LANES >= start, piece, partial)
                if stop >= (block + 1) * LANES:
                    unscaled[c, :, block * LANES : (block + 1) * LANES] = piece
                else:
                    partial = piece

    def edge_keys(t, c):
        here = pl.ds(pl.multiple_of(c * part, part), part)
        keys = pl.ds(pl.multiple_of(jnp.where(t == 0, 0, rows + EDGE), EDGE), EDGE)
        whole = at * tiles + t
        absent = (whole == 0) | (whole == groups * tiles - 1)
        bias = jnp.where(absent, -jnp.inf, 0.0)
        fresh_here = refreshed_ref[0, t] == 1
        partial = None
        ahead = scores_of(0, t, here, keys)
        for h in range(heads):
            start, stop, a, b = head_blocks(h)
            scores = ahead + bias
            if h < heads - 1:
                ahead = scores_of(h + 1, t, here, keys)
            old_top = tops[c, h]
            top = jnp.maximum(old_top, jnp.max(scores, axis=-1, keepdims=True))
            expo = jnp.exp2((scores - top) * scale)
            shrink = jnp.exp2((old_top - top) * scale)
            total = totals[c, h] * shrink + jnp.sum(expo, axis=-1, keepdims=True)
            out = jnp.dot(
                expo.astype(jnp.bfloat16),
                value[t, keys, a * LANES : b * LANES],
                preferred_element_type=jnp.float32,
            )
            inverse = 1.0 / total
            for block in range(a, b):
                piece = out[:, (block - a) * LANES : (block - a + 1) * LANES]
                piece = piece + unscaled[c, :, block * LANES : (block + 1) * LANES] * shrink
                piece = piece * inverse
                if start > block * LANES:
                    piece = jnp.where(lane + block * LANES >= start, piece, partial)
                if stop >= (block + 1) * LANES:
                    old = cached[t, here, block * LANES : (block + 1) * LANES]
                    spatial[:, block * LANES : (block + 1) * LANES] = jnp.where(
                        fresh_here, piece.astype(jnp.bfloat16), old
                    )
                else:
                    partial = piece
        projected = jnp.dot(spatial[...], out_weight[...], preferred_element_type=jnp.float32)
        hid = (latent[t, here].astype(jnp.float32) + projected).astype(jnp.bfloat16)
        hidden[t, c] = hid.reshape(frames, piece_rows, width)
        hid32 = hid.astype(jnp.float32)
        mean = jnp.mean(hid32 * hid32, axis=-1, keepdims=True)
        norm = (hid32 * lax.rsqrt(mean + 1e-06)).astype(jnp.bfloat16)
        normed[t, c] = norm.reshape(frames, piece_rows, width)
        for i in others:
            norm_copy(t, c, i, target_of(i)).start()
        hidden_copy(t, c).start()
        arrived[t, me, c] = normed[t, c, me]

    def spatial_tile(t, carry):
        def before(c, inner):
            own_keys(t, c)
            return inner

        def after(c, inner):
            edge_keys(t, c)
            return inner

        lax.fori_loop(0, PARTS, before, 0)

        @pl.when(t == 0)
        def _():
            for copy in loads[ready:early]:
                copy.wait()

        @pl.when(jnp.logical_and(has_above, t == 0))
        def _():
            for i in range(2):
                edge(i, 0, at - 1).wait_recv()

        @pl.when(jnp.logical_and(has_below, t == 0))
        def _():
            for i in range(2):
                edge(i, 0, at + 1).wait_send()

        @pl.when(jnp.logical_and(has_above, t == 0))
        def _():
            for i in range(2):
                edge(i, 1, at - 1).start()

        @pl.when(jnp.logical_and(has_below, t == tiles - 1))
        def _():
            for i in range(2):
                edge(i, 1, at + 1).wait_recv()

        lax.fori_loop(0, PARTS, after, 0)
        return carry

    lax.fori_loop(0, tiles, spatial_tile, 0)
    loads[early].wait()

    def temporal_tile(t, carry):
        for c in range(PARTS):
            for i in others:
                norm_in(t, c, i).wait_recv()
        block = arrived[t].reshape(frames * share, width)

        def project(j, c):
            w = temporal_weight[:, pl.ds(pl.multiple_of(j * width, LANES), width)]
            flat = jnp.dot(block, w, preferred_element_type=jnp.float32).astype(jnp.bfloat16)
            packed[j] = flat.reshape(frames, share, width)
            return c

        lax.fori_loop(0, 3, project, 0)
        for i in range(frames):
            f = target_of(i) if i < frames - 1 else me
            products = packed[0, f][None] * packed[1]
            scores = jnp.dot(
                products.reshape(frames * share, width),
                gather[...],
                preferred_element_type=jnp.float32,
            ).reshape(frames, share, LANES)
            scores = [
                jnp.where(jnp.abs(f - g) <= band, scores[g], -jnp.inf) for g in range(frames)
            ]
            top = functools.reduce(jnp.maximum, scores)
            expo = [jnp.exp2((s - top) * scale) for s in scores]
            inverse = 1.0 / functools.reduce(jnp.add, expo)
            weights = jnp.stack([(e * inverse).astype(jnp.bfloat16) for e in expo])
            wide = jnp.dot(
                weights.reshape(frames * share, LANES),
                spread[...],
                preferred_element_type=jnp.float32,
            ).reshape(frames, share, width)
            result = wide[0] * packed[2, 0].astype(jnp.float32)
            for g in range(1, frames):
                result = result + wide[g] * packed[2, g].astype(jnp.float32)
            attended[t, f] = result.astype(jnp.bfloat16).reshape(PARTS, piece_rows, width)
            if i < frames - 1:
                back_copy(t, i, f).start()
            else:
                own_copy(t).start()
        return carry

    lax.fori_loop(0, tiles, temporal_tile, 0)

    for t in range(tiles):
        for c in range(PARTS):
            hidden_copy(t, c).wait()
            for i in others:
                norm_copy(t, c, i, target_of(i)).wait_send()
        own_copy(t).wait()
        for i in others:
            back_copy(t, i, target_of(i)).wait_send()
            back_in(t, i).wait_recv()

    @pl.when(has_above)
    def _():
        for i in range(2):
            edge(i, 1, at - 1).wait_send()


def local(
    latent,
    query_rows,
    key_rows,
    value_rows,
    cached_out,
    refreshed,
    band_width,
    out_weight,
    temporal_weight,
):
    frame_count, tiles, rows, width = latent.shape
    assert frame_count == 1 and tiles == 2
    heads = band_width.shape[0]
    frames = lax.axis_size("frames")
    groups = lax.axis_size("space")
    share = rows // frames
    span = rows + 2 * EDGE
    bf16 = latent.dtype
    anywhere = pl.BlockSpec(memory_space=pl.ANY)
    scalars = pl.BlockSpec(memory_space=pltpu.SMEM)
    dma = pltpu.SemaphoreType.DMA
    piece = share // PARTS
    shape = (1, tiles, PARTS, frames, piece, width)
    hidden, temporal = pl.pallas_call(
        functools.partial(kernel, frames, groups, heads),
        out_shape=[jax.ShapeDtypeStruct(shape, bf16)] * 2,
        in_specs=[anywhere] * 5 + [scalars] * 2 + [anywhere] * 2,
        out_specs=[anywhere] * 2,
        scratch_shapes=[
            pltpu.VMEM((tiles, rows, width), bf16),
            pltpu.VMEM((tiles, span, width), bf16),
            pltpu.VMEM((tiles, span, width), bf16),
            pltpu.VMEM((tiles, rows, width), bf16),
            pltpu.VMEM((tiles, rows, width), bf16),
            pltpu.VMEM(out_weight.shape, bf16),
            pltpu.VMEM(temporal_weight.shape, bf16),
            pltpu.VMEM((rows // PARTS, width), bf16),
            pltpu.VMEM(shape[1:], bf16),
            pltpu.VMEM(shape[1:], bf16),
            pltpu.VMEM((tiles, frames, PARTS, piece, width), bf16),
            pltpu.VMEM((3, frames, share, width), bf16),
            pltpu.VMEM((tiles, frames, PARTS, piece, width), bf16),
            pltpu.VMEM((width, LANES), bf16),
            pltpu.VMEM((LANES, width), bf16),
            pltpu.VMEM((PARTS, heads, rows // PARTS, 1), jnp.float32),
            pltpu.VMEM((PARTS, heads, rows // PARTS, 1), jnp.float32),
            pltpu.VMEM((PARTS, rows // PARTS, width), jnp.float32),
            dma((3 * tiles + 4 * (tiles - 1) + 4,)),
            dma((2, 2)),
            dma((2, 2)),
            dma((tiles, PARTS, frames - 1)),
            dma((tiles, PARTS, frames - 1)),
            dma((tiles, frames - 1)),
            dma((tiles, frames - 1)),
            dma((tiles, PARTS)),
            dma((tiles,)),
        ],
        compiler_params=pltpu.CompilerParams(
            collective_id=0, has_side_effects=True, vmem_limit_bytes=60 * 1024 * 1024
        ),
        cost_estimate=pl.CostEstimate(
            flops=12 * 10**9, bytes_accessed=18 * 10**6, transcendentals=3 * 10**6
        ),
    )(
        latent,
        query_rows,
        key_rows,
        value_rows,
        cached_out,
        refreshed,
        band_width,
        out_weight,
        temporal_weight,
    )
    mixed = hidden.astype(jnp.float32) + temporal.astype(jnp.float32)
    return mixed.astype(jnp.bfloat16).reshape(latent.shape)


def solution(mesh):
    return jax.shard_map(
        local,
        mesh=mesh,
        in_specs=(
            P("frames", "space", None, None),
            P("frames", "space", None, None),
            P("frames", "space", None, None),
            P("frames", "space", None, None),
            P("frames", "space", None, None),
            P("frames", "space"),
            P(),
            P(),
            P(),
        ),
        out_specs=P("frames", "space", None, None),
        check_vma=False,
    )
```

```python
import functools
import math

import jax
import jax.numpy as jnp
from jax import lax
from jax.experimental import pallas as pl
from jax.experimental.pallas import tpu as pltpu
from jax.sharding import PartitionSpec as P

EDGE = 64
PARTS = 1
LANES = 128
MESH = pl.DeviceIdType.MESH


def kernel(
    frames,
    groups,
    heads,
    latent_hbm,
    query_hbm,
    key_hbm,
    value_hbm,
    cached_hbm,
    refreshed_ref,
    band_ref,
    out_weight_hbm,
    temporal_weight_hbm,
    hidden_out,
    temporal_out,
    query,
    key,
    value,
    latent,
    cached,
    out_weight,
    temporal_weight,
    spatial,
    hidden,
    normed,
    arrived,
    packed,
    attended,
    gather,
    spread,
    load_sem,
    edge_send,
    edge_recv,
    norm_send,
    norm_recv,
    back_send,
    back_recv,
    hidden_sem,
    own_sem,
):
    _, tiles, rows, width = latent_hbm.shape
    share = rows // frames
    part = rows // PARTS
    piece_rows = part // frames
    span = rows + 2 * EDGE
    head_dim = width // heads
    me = lax.axis_index("frames")
    at = lax.axis_index("space")
    chips = frames // 2
    chip, core = me // 2, lax.rem(me, 2)
    steps = [(k, j) for k in range(1, chips) for j in range(2)] + [(0, 1)]

    def target_of(i):
        k, j = steps[i]
        return lax.rem(chip + k, chips) * 2 + lax.rem(core + j, 2)

    def source_of(i):
        k, j = steps[i]
        return lax.rem(chip + chips - k, chips) * 2 + lax.rem(core + j, 2)

    others = range(frames - 1)
    has_above = at > 0
    has_below = at < groups - 1

    barrier = pltpu.get_barrier_semaphore()
    for i in others:
        pl.semaphore_signal(
            barrier, inc=1, device_id={"frames": target_of(i)}, device_id_type=MESH
        )

    @pl.when(has_above)
    def _():
        pl.semaphore_signal(barrier, inc=1, device_id={"space": at - 1}, device_id_type=MESH)

    @pl.when(has_below)
    def _():
        pl.semaphore_signal(barrier, inc=1, device_id={"space": at + 1}, device_id_type=MESH)

    loads = []

    def load(src, dst):
        copy = pltpu.make_async_copy(src, dst, load_sem.at[len(loads)])
        copy.start()
        loads.append(copy)

    for t in range(tiles):
        load(query_hbm.at[0, t], query.at[t])
        for src, dst in ((key_hbm, key), (value_hbm, value)):
            load(src.at[0, t], dst.at[t, pl.ds(EDGE, rows)])
            if t > 0:
                load(src.at[0, t - 1, pl.ds(rows - EDGE, EDGE)], dst.at[t, pl.ds(0, EDGE)])
            if t < tiles - 1:
                load(src.at[0, t + 1, pl.ds(0, EDGE)], dst.at[t, pl.ds(rows + EDGE, EDGE)])

    peers = frames - 1 + jnp.where(has_above, 1, 0) + jnp.where(has_below, 1, 0)
    pl.semaphore_wait(barrier, peers)

    def edge(i, which, target):
        src, dst = ((key_hbm, key), (value_hbm, value))[i]
        if which == 0:
            source = src.at[0, tiles - 1, pl.ds(rows - EDGE, EDGE)]
            place = dst.at[0, pl.ds(0, EDGE)]
        else:
            source = src.at[0, 0, pl.ds(0, EDGE)]
            place = dst.at[tiles - 1, pl.ds(rows + EDGE, EDGE)]
        return pltpu.make_async_remote_copy(
            src_ref=source,
            dst_ref=place,
            send_sem=edge_send.at[which, i],
            recv_sem=edge_recv.at[which, i],
            device_id={"space": target},
            device_id_type=MESH,
        )

    @pl.when(has_below)
    def _():
        for i in range(2):
            edge(i, 0, at + 1).start()

    load(cached_hbm.at[0], cached)
    load(latent_hbm.at[0], latent)
    load(out_weight_hbm, out_weight)
    early = len(loads)
    load(temporal_weight_hbm, temporal_weight)

    @pl.when(jnp.logical_not(has_above))
    def _():
        for dst in (key, value):
            dst[0, pl.ds(0, EDGE)] = jnp.zeros((EDGE, width), dst.dtype)

    @pl.when(jnp.logical_not(has_below))
    def _():
        for dst in (key, value):
            dst[tiles - 1, pl.ds(rows + EDGE, EDGE)] = jnp.zeros((EDGE, width), dst.dtype)

    column = lax.broadcasted_iota(jnp.int32, (width, LANES), 0)
    first = lax.broadcasted_iota(jnp.int32, (width, LANES), 1) * head_dim
    inside = jnp.where((column >= first) & (column < first + head_dim), 1.0, 0.0)
    gather[...] = inside.astype(jnp.bfloat16)
    column = lax.broadcasted_iota(jnp.int32, (LANES, width), 1)
    first = lax.broadcasted_iota(jnp.int32, (LANES, width), 0) * head_dim
    inside = jnp.where((column >= first) & (column < first + head_dim), 1.0, 0.0)
    spread[...] = inside.astype(jnp.bfloat16)
    lane = lax.broadcasted_iota(jnp.int32, (1, LANES), 1)
    band = jnp.zeros((1, LANES), jnp.int32)
    for h in range(heads):
        band = jnp.where(lane == h, band_ref[h], band)

    for copy in loads[:early]:
        copy.wait()

    @pl.when(has_above)
    def _():
        for i in range(2):
            edge(i, 0, at - 1).wait_recv()

    @pl.when(has_below)
    def _():
        for i in range(2):
            edge(i, 0, at + 1).wait_send()

    @pl.when(has_above)
    def _():
        for i in range(2):
            edge(i, 1, at - 1).start()

    scale = math.log2(math.e) / math.sqrt(head_dim)
    position = lax.broadcasted_iota(jnp.int32, (1, span), 1)

    def norm_copy(t, c, i, peer):
        return pltpu.make_async_remote_copy(
            src_ref=normed.at[t, c, peer],
            dst_ref=arrived.at[t, me, c],
            send_sem=norm_send.at[t, c, i],
            recv_sem=norm_recv.at[t, c, i],
            device_id={"frames": peer},
            device_id_type=MESH,
        )

    def norm_in(t, c, i):
        sender = source_of(i)
        return pltpu.make_async_remote_copy(
            src_ref=normed.at[t, c, sender],
            dst_ref=arrived.at[t, sender, c],
            send_sem=norm_send.at[t, c, i],
            recv_sem=norm_recv.at[t, c, i],
            device_id={"frames": sender},
            device_id_type=MESH,
        )

    def back_copy(t, i, peer):
        return pltpu.make_async_remote_copy(
            src_ref=attended.at[t, peer],
            dst_ref=temporal_out.at[0, t, :, me],
            send_sem=back_send.at[t, i],
            recv_sem=back_recv.at[t, i],
            device_id={"frames": peer},
            device_id_type=MESH,
        )

    def back_in(t, i):
        owner = source_of(i)
        return pltpu.make_async_remote_copy(
            src_ref=attended.at[t, owner],
            dst_ref=temporal_out.at[0, t, :, owner],
            send_sem=back_send.at[t, i],
            recv_sem=back_recv.at[t, i],
            device_id={"frames": owner},
            device_id_type=MESH,
        )

    def own_copy(t):
        return pltpu.make_async_copy(
            attended.at[t, me], temporal_out.at[0, t, :, me], own_sem.at[t]
        )

    def hidden_copy(t, c):
        return pltpu.make_async_copy(
            hidden.at[t, c], hidden_out.at[0, t, c], hidden_sem.at[t, c]
        )

    def head_blocks(h):
        start, stop = h * head_dim, (h + 1) * head_dim
        return start, stop, start // LANES, -(-stop // LANES)

    def spatial_part(n, carry):
        t, c = n // PARTS, lax.rem(n, PARTS)

        @pl.when(jnp.logical_and(has_below, n == (tiles - 1) * PARTS))
        def _():
            for i in range(2):
                edge(i, 1, at + 1).wait_recv()

        here = pl.ds(pl.multiple_of(c * part, part), part)
        whole = at * tiles + t
        low = jnp.where(whole == 0, EDGE, 0)
        high = jnp.where(whole == groups * tiles - 1, rows + EDGE, span)
        bias = jnp.where((position >= low) & (position < high), 0.0, -jnp.inf)
        fresh_here = refreshed_ref[0, t] == 1

        def scores_of(h):
            start, stop, a, b = head_blocks(h)
            cols = slice(a * LANES, b * LANES)
            at_col = lax.broadcasted_iota(jnp.int32, (1, (b - a) * LANES), 1) + a * LANES
            mine = (at_col >= start) & (at_col < stop)
            q = query[t, here, cols] * jnp.where(mine, 1.0, 0.0).astype(jnp.bfloat16)
            return lax.dot_general(
                q, key[t, :, cols], (((1,), (1,)), ((), ())), preferred_element_type=jnp.float32
            )

        partial = None
        ahead = scores_of(0)
        for h in range(heads):
            start, stop, a, b = head_blocks(h)
            scores = ahead + bias
            if h < heads - 1:
                ahead = scores_of(h + 1)
            top = jnp.max(scores, axis=-1, keepdims=True)
            expo = jnp.exp2((scores - top) * scale)
            total = jnp.sum(expo, axis=-1, keepdims=True)
            out = jnp.dot(
                expo.astype(jnp.bfloat16),
                value[t, :, a * LANES : b * LANES],
                preferred_element_type=jnp.float32,
            )
            out = out * (1.0 / total)
            for block in range(a, b):
                piece = out[:, (block - a) * LANES : (block - a + 1) * LANES]
                if start > block * LANES:
                    piece = jnp.where(lane + block * LANES >= start, piece, partial)
                if stop >= (block + 1) * LANES:
                    old = cached[t, here, block * LANES : (block + 1) * LANES]
                    spatial[:, block * LANES : (block + 1) * LANES] = jnp.where(
                        fresh_here, piece.astype(jnp.bfloat16), old
                    )
                else:
                    partial = piece
        projected = jnp.dot(spatial[...], out_weight[...], preferred_element_type=jnp.float32)
        hid = (latent[t, here].astype(jnp.float32) + projected).astype(jnp.bfloat16)
        hidden[t, c] = hid.reshape(frames, piece_rows, width)
        hid32 = hid.astype(jnp.float32)
        mean = jnp.mean(hid32 * hid32, axis=-1, keepdims=True)
        norm = (hid32 * lax.rsqrt(mean + 1e-06)).astype(jnp.bfloat16)
        normed[t, c] = norm.reshape(frames, piece_rows, width)
        for i in others:
            norm_copy(t, c, i, target_of(i)).start()
        hidden_copy(t, c).start()
        arrived[t, me, c] = normed[t, c, me]
        return carry

    lax.fori_loop(0, tiles * PARTS, spatial_part, 0)
    loads[early].wait()

    def temporal_tile(t, carry):
        for c in range(PARTS):
            for i in others:
                norm_in(t, c, i).wait_recv()
        block = arrived[t].reshape(frames * share, width)

        def project(j, c):
            w = temporal_weight[:, pl.ds(pl.multiple_of(j * width, LANES), width)]
            flat = jnp.dot(block, w, preferred_element_type=jnp.float32).astype(jnp.bfloat16)
            packed[j] = flat.reshape(frames, share, width)
            return c

        lax.fori_loop(0, 3, project, 0)
        for i in range(frames):
            f = target_of(i) if i < frames - 1 else me
            products = packed[0, f][None] * packed[1]
            scores = jnp.dot(
                products.reshape(frames * share, width),
                gather[...],
                preferred_element_type=jnp.float32,
            ).reshape(frames, share, LANES)
            scores = [
                jnp.where(jnp.abs(f - g) <= band, scores[g], -jnp.inf) for g in range(frames)
            ]
            top = functools.reduce(jnp.maximum, scores)
            expo = [jnp.exp2((s - top) * scale) for s in scores]
            inverse = 1.0 / functools.reduce(jnp.add, expo)
            weights = jnp.stack([(e * inverse).astype(jnp.bfloat16) for e in expo])
            wide = jnp.dot(
                weights.reshape(frames * share, LANES),
                spread[...],
                preferred_element_type=jnp.float32,
            ).reshape(frames, share, width)
            result = wide[0] * packed[2, 0].astype(jnp.float32)
            for g in range(1, frames):
                result = result + wide[g] * packed[2, g].astype(jnp.float32)
            attended[t, f] = result.astype(jnp.bfloat16).reshape(PARTS, piece_rows, width)
            if i < frames - 1:
                back_copy(t, i, f).start()
            else:
                own_copy(t).start()
        return carry

    lax.fori_loop(0, tiles, temporal_tile, 0)

    for t in range(tiles):
        for c in range(PARTS):
            hidden_copy(t, c).wait()
            for i in others:
                norm_copy(t, c, i, target_of(i)).wait_send()
        own_copy(t).wait()
        for i in others:
            back_copy(t, i, target_of(i)).wait_send()
            back_in(t, i).wait_recv()

    @pl.when(has_above)
    def _():
        for i in range(2):
            edge(i, 1, at - 1).wait_send()


def local(
    latent,
    query_rows,
    key_rows,
    value_rows,
    cached_out,
    refreshed,
    band_width,
    out_weight,
    temporal_weight,
):
    frame_count, tiles, rows, width = latent.shape
    assert frame_count == 1
    heads = band_width.shape[0]
    frames = lax.axis_size("frames")
    groups = lax.axis_size("space")
    share = rows // frames
    span = rows + 2 * EDGE
    bf16 = latent.dtype
    anywhere = pl.BlockSpec(memory_space=pl.ANY)
    scalars = pl.BlockSpec(memory_space=pltpu.SMEM)
    dma = pltpu.SemaphoreType.DMA
    piece = share // PARTS
    shape = (1, tiles, PARTS, frames, piece, width)
    hidden, temporal = pl.pallas_call(
        functools.partial(kernel, frames, groups, heads),
        out_shape=[jax.ShapeDtypeStruct(shape, bf16)] * 2,
        in_specs=[anywhere] * 5 + [scalars] * 2 + [anywhere] * 2,
        out_specs=[anywhere] * 2,
        scratch_shapes=[
            pltpu.VMEM((tiles, rows, width), bf16),
            pltpu.VMEM((tiles, span, width), bf16),
            pltpu.VMEM((tiles, span, width), bf16),
            pltpu.VMEM((tiles, rows, width), bf16),
            pltpu.VMEM((tiles, rows, width), bf16),
            pltpu.VMEM(out_weight.shape, bf16),
            pltpu.VMEM(temporal_weight.shape, bf16),
            pltpu.VMEM((rows // PARTS, width), bf16),
            pltpu.VMEM(shape[1:], bf16),
            pltpu.VMEM(shape[1:], bf16),
            pltpu.VMEM((tiles, frames, PARTS, piece, width), bf16),
            pltpu.VMEM((3, frames, share, width), bf16),
            pltpu.VMEM((tiles, frames, PARTS, piece, width), bf16),
            pltpu.VMEM((width, LANES), bf16),
            pltpu.VMEM((LANES, width), bf16),
            dma((3 * tiles + 4 * (tiles - 1) + 4,)),
            dma((2, 2)),
            dma((2, 2)),
            dma((tiles, PARTS, frames - 1)),
            dma((tiles, PARTS, frames - 1)),
            dma((tiles, frames - 1)),
            dma((tiles, frames - 1)),
            dma((tiles, PARTS)),
            dma((tiles,)),
        ],
        compiler_params=pltpu.CompilerParams(
            collective_id=0, has_side_effects=True, vmem_limit_bytes=60 * 1024 * 1024
        ),
        cost_estimate=pl.CostEstimate(
            flops=12 * 10**9, bytes_accessed=18 * 10**6, transcendentals=3 * 10**6
        ),
    )(
        latent,
        query_rows,
        key_rows,
        value_rows,
        cached_out,
        refreshed,
        band_width,
        out_weight,
        temporal_weight,
    )
    mixed = hidden.astype(jnp.float32) + temporal.astype(jnp.float32)
    return mixed.astype(jnp.bfloat16).reshape(latent.shape)


def solution(mesh):
    return jax.shard_map(
        local,
        mesh=mesh,
        in_specs=(
            P("frames", "space", None, None),
            P("frames", "space", None, None),
            P("frames", "space", None, None),
            P("frames", "space", None, None),
            P("frames", "space", None, None),
            P("frames", "space"),
            P(),
            P(),
            P(),
        ),
        out_specs=P("frames", "space", None, None),
        check_vma=False,
    )
```
